32 devices in a mesh: lag: 4 (over z), probe: 4 (over y, x), sketch: 2 (over core).
Axes of the slice: x: 2, y: 2, z: 4, core: 2. Of those that a mesh axis runs over, the one named last changes fastest.
Arguments:
- markov: bfloat16 [16, 32, 8192], P('lag', None, ('probe', 'sketch')), may hold values from -36 to 36
- test_matrix: bfloat16 [4, 32, 256], P('lag', None, 'sketch'), may hold values from -0.5 to 0.5
Outputs:
- sketch_out: bfloat16 [16, 8192, 256], P('lag', 'probe', 'sketch')
The draws below stay inside these ranges and needn't reach their ends.
All inputs are finite; a program needn't handle non-finite values.
Results may differ from the reference program's by a relative error of at most 0.0004.
Values may be sent and summed in bfloat16 or wider, within the bound.
A program may use at most 64 MiB of HBM per device.

```python
import math
import jax
import jax.numpy as jnp
from jax import lax

P_SIZE = 8192
M_IN = 32
R = 256
S_DEV = 4
STEPS = 16
LAGS = 4
N_LAG = 4


def draw_markov(key, part):
    keys = jax.random.split(jax.random.fold_in(key, 17), 4)
    times = jnp.arange(STEPS, dtype=jnp.float32) / STEPS
    envelope = jnp.exp(-1.2 * times)
    base = jnp.clip(jax.random.normal(keys[0], (STEPS, M_IN, P_SIZE), jnp.float32), -5.0, 5.0)
    probe_scale = jnp.exp(jax.random.uniform(keys[1], (P_SIZE,), jnp.float32, 0.0, math.log(10.0)))
    input_scale = jnp.exp(jax.random.uniform(keys[2], (M_IN,), jnp.float32, 0.0, math.log(3.0)))
    rough = jnp.exp(jax.random.uniform(keys[3], (STEPS,), jnp.float32, -0.35, 0.35))
    values = base * (envelope * rough)[:, None, None] * input_scale[None, :, None] * probe_scale[None, None, :] / 6.0
    return values.astype(jnp.bfloat16)


def block_scale(own_key, shape, cuts, low, top_value):
    gain, own = 1.0, jax.random.fold_in(own_key, 6)
    for axis_at, blocks in cuts:
        draws = jnp.exp(jax.random.uniform(jax.random.fold_in(own, axis_at), (blocks,), jnp.float32, low / len(cuts), top_value / len(cuts)))
        gain = gain * jnp.repeat(draws, shape[axis_at] // blocks).reshape([-1 if axis == axis_at else 1 for axis in range(len(shape))])
    return gain


def noise(own_key, shape, width, most, shards=(), held_as=jnp.bfloat16):
    entries = jax.random.normal(own_key, shape, jnp.float32) * width
    if len(shards) > 0:
        entries = block_scale(own_key, shape, shards, -0.22, 0.18) * entries
    return jnp.clip(entries, min=-most, max=most).astype(held_as)


def setup_inputs(seed: int = 0) -> dict:
    key_list = jax.random.split(jax.random.key(seed), 3)
    return {
        "markov": draw_markov(jax.random.fold_in(key_list[2], 71), 0),
        "test_matrix": noise(key_list[1], (LAGS, M_IN, R), (LAGS * M_IN) ** -0.5, 0.5, ((0, 4), (2, 2))),
    }


def reference(markov, test_matrix):
    step_count = markov.shape[0]
    lag_count = test_matrix.shape[0]
    padded = jnp.concatenate([markov, jnp.zeros((lag_count, M_IN, P_SIZE), markov.dtype)], axis=0)
    flat_matrix = test_matrix.reshape(lag_count * M_IN, R)

    def group_rows(group_index):
        window = lax.dynamic_slice_in_dim(padded, group_index * S_DEV, S_DEV + lag_count, 0)
        pieces = [jnp.dot(window[row_index:row_index + lag_count].reshape(lag_count * M_IN, P_SIZE).T, flat_matrix, preferred_element_type=jnp.float32) for row_index in range(S_DEV)]
        return jnp.stack(pieces)
    sketch_raw = lax.map(group_rows, jnp.arange(N_LAG, dtype=jnp.int32)).reshape(step_count, P_SIZE, R)
    column_sums = lax.optimization_barrier(jnp.sum(sketch_raw * sketch_raw, axis=(0, 1)))
    factor = lax.rsqrt(column_sums / (step_count * P_SIZE) + 1e-06)
    return (sketch_raw * factor).astype(jnp.bfloat16)
```

```python
import functools

import jax
import jax.numpy as jnp
from jax import lax
from jax.experimental import pallas as pl
from jax.experimental.pallas import tpu as pltpu
from jax.sharding import PartitionSpec as P

MESH = pl.DeviceIdType.MESH
UNROLL = 32


def loop(count, body):
    if count <= UNROLL:
        for index in range(count):
            body(index)
    else:
        def step(index, carry):
            body(index)
            return carry
        lax.fori_loop(0, count, step, 0)


def plan(step_count, lag_total):
    steps = step_count + lag_total - 1
    blocks = (steps - 1) // step_count
    pieces = []
    for ahead in range(1, blocks + 1):
        used = min(step_count, steps - ahead * step_count)
        if blocks == 1:
            pieces += [(ahead, at, 1) for at in range(used)]
        else:
            pieces.append((ahead, 0, used))
    return steps, pieces


def gather_kernel(
    sizes, markov, matrix, raw, factor,
    window, held, weights, sums,
    own_sem, matrix_own_sem, matrix_send, matrix_recv,
    pair_send, pair_recv, lag_send, lag_recv, next_send, next_recv, sum_send, sum_recv,
):
    n_lag, n_probe, n_sketch = sizes
    step_count, input_count, half = markov.shape
    matrix_rows = matrix.shape[0]
    columns = matrix.shape[2]
    lag_total = matrix_rows * n_lag
    steps, pieces = plan(step_count, lag_total)
    lag = lax.axis_index("lag")
    probe = lax.axis_index("probe")
    sketch = lax.axis_index("sketch")
    flat = lag * n_probe + probe
    peers = n_lag * n_probe - 1

    def peer(index):
        other = lax.rem(flat + 1 + index, peers + 1)
        return {
            "lag": lax.div(other, n_probe),
            "probe": lax.rem(other, n_probe),
            "sketch": sketch,
        }

    def partner(index):
        return {"lag": lag, "probe": probe, "sketch": lax.rem(sketch + 1 + index, n_sketch)}

    def lag_peer(index):
        return {"lag": lax.rem(lag + 1 + index, n_lag), "probe": probe, "sketch": sketch}

    barrier = pltpu.get_barrier_semaphore()

    def greet(index):
        pl.semaphore_signal(barrier, inc=1, device_id=peer(index), device_id_type=MESH)

    for index in range(n_sketch - 1):
        pl.semaphore_signal(barrier, inc=1, device_id=partner(index), device_id_type=MESH)
    loop(peers, greet)

    own = pltpu.make_async_copy(markov, window.at[sketch, pl.ds(0, step_count)], own_sem)
    own.start()
    matrix_own = pltpu.make_async_copy(
        matrix, held.at[pl.ds(lag * matrix_rows, matrix_rows)], matrix_own_sem
    )
    matrix_own.start()
    weights[...] = jnp.zeros_like(weights)
    for ahead, at, count in pieces:
        @pl.when(lag + ahead >= n_lag)
        def _():
            place = pl.ds(ahead * step_count + at, count)
            window[:, place] = jnp.zeros((n_sketch, count, input_count, half), window.dtype)

    pl.semaphore_wait(barrier, peers + n_sketch - 1)

    def lag_copy(number):
        ahead, at, count = pieces[number]
        return pltpu.make_async_remote_copy(
            src_ref=markov.at[pl.ds(at, count)],
            dst_ref=window.at[sketch, pl.ds(ahead * step_count + at, count)],
            send_sem=lag_send.at[number],
            recv_sem=lag_recv.at[number],
            device_id={"lag": lax.max(lag - ahead, 0), "probe": probe, "sketch": sketch},
            device_id_type=MESH,
        )

    def pair_copy(index):
        return pltpu.make_async_remote_copy(
            src_ref=markov,
            dst_ref=window.at[sketch, pl.ds(0, step_count)],
            send_sem=pair_send.at[index],
            recv_sem=pair_recv.at[index],
            device_id=partner(index),
            device_id_type=MESH,
        )

    def next_copy(number, index):
        ahead, at, count = pieces[number]
        place = window.at[sketch, pl.ds(ahead * step_count + at, count)]
        return pltpu.make_async_remote_copy(
            src_ref=place,
            dst_ref=place,
            send_sem=next_send.at[number, index],
            recv_sem=next_recv.at[number, index],
            device_id=partner(index),
            device_id_type=MESH,
        )

    def matrix_copy(index):
        return pltpu.make_async_remote_copy(
            src_ref=matrix,
            dst_ref=held.at[pl.ds(lag * matrix_rows, matrix_rows)],
            send_sem=matrix_send,
            recv_sem=matrix_recv,
            device_id=lag_peer(index),
            device_id_type=MESH,
        )

    for number in range(len(pieces)):
        @pl.when(lag >= pieces[number][0])
        def _():
            lag_copy(number).start()
        if number == 0:
            loop(n_lag - 1, lambda index: matrix_copy(index).start())
            for index in range(n_sketch - 1):
                pair_copy(index).start()

    matrix_own.wait()
    if n_lag > 1:
        arrived = held.at[pl.ds(0, (n_lag - 1) * matrix_rows)]
        pltpu.make_async_copy(arrived, arrived, matrix_recv).wait()
        pltpu.make_async_copy(arrived, arrived, matrix_send).wait()
    for row in range(step_count):
        weights[pl.ds(row * input_count, lag_total * input_count), row * columns:(row + 1) * columns] = (
            held[...].reshape(lag_total * input_count, columns)
        )

    def forward(number):
        @pl.when(lag + pieces[number][0] < n_lag)
        def _():
            lag_copy(number).wait_recv()
            for index in range(n_sketch - 1):
                next_copy(number, index).start()

    def landed(number):
        @pl.when(lag + pieces[number][0] < n_lag)
        def _():
            for index in range(n_sketch - 1):
                next_copy(number, index).wait()

    tile = min(256, half)
    group = 2 if step_count % 2 == 0 else 1

    def compute(first, total):
        depth = (lag_total + group - 1) * input_count
        weight = weights[pl.ds(first * input_count, depth), first * columns:(first + group) * columns]
        for side in range(n_sketch):
            def body(at, total):
                start = pl.multiple_of(at * tile, tile)
                block = window[side, pl.ds(first, lag_total + group - 1), :, pl.ds(start, tile)]
                product = lax.dot_general(
                    block.reshape(depth, tile), weight, (((0,), (0,)), ((), ())),
                    preferred_element_type=jnp.float32,
                )
                for row in range(group):
                    part = product[:, row * columns:(row + 1) * columns]
                    raw[first + row, pl.ds(side * half + start, tile), :] = part
                    total = total + jnp.sum((part * part).reshape(tile // 8, 8, columns), axis=0)
                return total
            total = lax.fori_loop(0, half // tile, body, total, unroll=depth <= 512)
        return total

    own.wait()
    total = jnp.zeros((8, columns), jnp.float32)
    done = 0
    paired = False
    for first in range(0, step_count, group):
        need = first + group - 1 + lag_total
        ready = done
        while ready < len(pieces) and pieces[ready][0] * step_count + pieces[ready][1] < need:
            forward(ready)
            ready += 1
        if not paired:
            for index in range(n_sketch - 1):
                pair_copy(index).wait()
            paired = True
        for number in range(done, ready):
            landed(number)
        done = ready
        total = compute(first, total)

    sums[pl.ds(flat, 1), :] = jnp.sum(total, axis=0, keepdims=True)

    def sum_copy(index):
        place = sums.at[pl.ds(flat, 1)]
        return pltpu.make_async_remote_copy(
            src_ref=place,
            dst_ref=place,
            send_sem=sum_send,
            recv_sem=sum_recv,
            device_id=peer(index),
            device_id_type=MESH,
        )

    loop(peers, lambda index: sum_copy(index).start())
    for number in range(len(pieces)):
        @pl.when(lag >= pieces[number][0])
        def _():
            lag_copy(number).wait_send()
    if peers:
        arrived = sums.at[pl.ds(0, peers)]
        pltpu.make_async_copy(arrived, arrived, sum_recv).wait()
        pltpu.make_async_copy(arrived, arrived, sum_send).wait()
    cells = step_count * n_lag * half * n_sketch * n_probe
    mean = jnp.sum(sums[...], axis=0, keepdims=True) / cells
    factor[...] = jnp.broadcast_to(lax.rsqrt(mean + 1e-06), factor.shape)


def local(sizes, markov, test_matrix):
    n_lag, n_probe, n_sketch = sizes
    step_count, input_count, half = markov.shape
    matrix_rows, _, columns = test_matrix.shape
    lag_total = matrix_rows * n_lag
    steps, pieces = plan(step_count, lag_total)
    count = max(len(pieces), 1)
    pairs = max(n_sketch - 1, 1)
    probes = half * n_sketch
    dma = pltpu.SemaphoreType.DMA
    raw, factor = pl.pallas_call(
        functools.partial(gather_kernel, sizes),
        out_shape=[
            pltpu.VMEM((step_count, probes, columns), jnp.float32),
            pltpu.VMEM((8, columns), jnp.float32),
        ],
        in_specs=[pl.BlockSpec(memory_space=pltpu.HBM)] * 2,
        out_specs=[pl.BlockSpec(memory_space=pltpu.VMEM)] * 2,
        scratch_shapes=[
            pltpu.VMEM((n_sketch, steps, input_count, half), jnp.bfloat16),
            pltpu.VMEM((lag_total, input_count, columns), jnp.bfloat16),
            pltpu.VMEM((steps * input_count, step_count * columns), jnp.bfloat16),
            pltpu.VMEM((n_lag * n_probe, columns), jnp.float32),
            dma, dma, dma, dma,
            dma((pairs,)), dma((pairs,)),
            dma((count,)), dma((count,)),
            dma((count, pairs)), dma((count, pairs)),
            dma, dma,
        ],
        compiler_params=pltpu.CompilerParams(
            collective_id=0, has_side_effects=True, vmem_limit_bytes=40 * 1024 * 1024
        ),
    )(markov, test_matrix)
    return (raw * factor[0]).astype(jnp.bfloat16)


def solution(mesh):
    sizes = tuple(mesh.shape[name] for name in ("lag", "probe", "sketch"))
    return jax.shard_map(
        functools.partial(local, sizes),
        mesh=mesh,
        in_specs=(P("lag", None, ("probe", "sketch")), P("lag", None, "sketch")),
        out_specs=P("lag", "probe", "sketch"),
        check_vma=False,
    )
```

```python
import functools

import jax
import jax.numpy as jnp
from jax import lax
from jax.experimental import pallas as pl
from jax.experimental.pallas import tpu as pltpu
from jax.sharding import PartitionSpec as P

MESH = pl.DeviceIdType.MESH
UNROLL = 32


def loop(count, body):
    if count <= UNROLL:
        for index in range(count):
            body(index)
    else:
        def step(index, carry):
            body(index)
            return carry
        lax.fori_loop(0, count, step, 0)


def plan(step_count, lag_total):
    steps = step_count + lag_total - 1
    blocks = (steps - 1) // step_count
    pieces = []
    for ahead in range(1, blocks + 1):
        used = min(step_count, steps - ahead * step_count)
        if blocks == 1:
            pieces += [(ahead, at, 1) for at in range(used)]
        else:
            pieces.append((ahead, 0, used))
    return steps, pieces


def gather_kernel(
    sizes, markov, matrix, raw, factor,
    window, held, weights, sums,
    own_sem, matrix_own_sem, matrix_send, matrix_recv,
    pair_send, pair_recv, lag_send, lag_recv, next_send, next_recv, sum_send, sum_recv,
):
    n_lag, n_probe, n_sketch = sizes
    step_count, input_count, half = markov.shape
    matrix_rows = matrix.shape[0]
    columns = matrix.shape[2]
    lag_total = matrix_rows * n_lag
    steps, pieces = plan(step_count, lag_total)
    lag = lax.axis_index("lag")
    probe = lax.axis_index("probe")
    sketch = lax.axis_index("sketch")
    flat = lag * n_probe + probe
    peers = n_lag * n_probe - 1

    def peer(index):
        other = lax.rem(flat + 1 + index, peers + 1)
        return {
            "lag": lax.div(other, n_probe),
            "probe": lax.rem(other, n_probe),
            "sketch": sketch,
        }

    def partner(index):
        return {"lag": lag, "probe": probe, "sketch": lax.rem(sketch + 1 + index, n_sketch)}

    def lag_peer(index):
        return {"lag": lax.rem(lag + 1 + index, n_lag), "probe": probe, "sketch": sketch}

    barrier = pltpu.get_barrier_semaphore()

    def greet(index):
        pl.semaphore_signal(barrier, inc=1, device_id=peer(index), device_id_type=MESH)

    for index in range(n_sketch - 1):
        pl.semaphore_signal(barrier, inc=1, device_id=partner(index), device_id_type=MESH)
    loop(peers, greet)

    own = pltpu.make_async_copy(markov, window.at[sketch, pl.ds(0, step_count)], own_sem)
    own.start()
    matrix_own = pltpu.make_async_copy(
        matrix, held.at[pl.ds(lag * matrix_rows, matrix_rows)], matrix_own_sem
    )
    matrix_own.start()
    weights[...] = jnp.zeros_like(weights)
    for ahead, at, count in pieces:
        @pl.when(lag + ahead >= n_lag)
        def _():
            place = pl.ds(ahead * step_count + at, count)
            window[:, place] = jnp.zeros((n_sketch, count, input_count, half), window.dtype)

    pl.semaphore_wait(barrier, peers + n_sketch - 1)

    def lag_copy(number):
        ahead, at, count = pieces[number]
        return pltpu.make_async_remote_copy(
            src_ref=markov.at[pl.ds(at, count)],
            dst_ref=window.at[sketch, pl.ds(ahead * step_count + at, count)],
            send_sem=lag_send.at[number],
            recv_sem=lag_recv.at[number],
            device_id={"lag": lax.max(lag - ahead, 0), "probe": probe, "sketch": sketch},
            device_id_type=MESH,
        )

    def pair_copy(index):
        return pltpu.make_async_remote_copy(
            src_ref=markov,
            dst_ref=window.at[sketch, pl.ds(0, step_count)],
            send_sem=pair_send.at[index],
            recv_sem=pair_recv.at[index],
            device_id=partner(index),
            device_id_type=MESH,
        )

    def next_copy(number, index):
        ahead, at, count = pieces[number]
        place = window.at[sketch, pl.ds(ahead * step_count + at, count)]
        return pltpu.make_async_remote_copy(
            src_ref=place,
            dst_ref=place,
            send_sem=next_send.at[number, index],
            recv_sem=next_recv.at[number, index],
            device_id=partner(index),
            device_id_type=MESH,
        )

    def matrix_copy(index):
        return pltpu.make_async_remote_copy(
            src_ref=matrix,
            dst_ref=held.at[pl.ds(lag * matrix_rows, matrix_rows)],
            send_sem=matrix_send,
            recv_sem=matrix_recv,
            device_id=lag_peer(index),
            device_id_type=MESH,
        )

    for number in range(len(pieces)):
        @pl.when(lag >= pieces[number][0])
        def _():
            lag_copy(number).start()
        if number == 0:
            loop(n_lag - 1, lambda index: matrix_copy(index).start())
            for index in range(n_sketch - 1):
                pair_copy(index).start()

    matrix_own.wait()
    if n_lag > 1:
        arrived = held.at[pl.ds(0, (n_lag - 1) * matrix_rows)]
        pltpu.make_async_copy(arrived, arrived, matrix_recv).wait()
        pltpu.make_async_copy(arrived, arrived, matrix_send).wait()
    for row in range(step_count):
        weights[pl.ds(row * input_count, lag_total * input_count), row * columns:(row + 1) * columns] = (
            held[...].reshape(lag_total * input_count, columns)
        )

    def forward(number):
        @pl.when(lag + pieces[number][0] < n_lag)
        def _():
            lag_copy(number).wait_recv()
            for index in range(n_sketch - 1):
                next_copy(number, index).start()

    def landed(number):
        @pl.when(lag + pieces[number][0] < n_lag)
        def _():
            for index in range(n_sketch - 1):
                next_copy(number, index).wait()

    tile = min(256, half)
    group = 2 if step_count % 2 == 0 else 1

    def compute(first, total):
        depth = (lag_total + group - 1) * input_count
        weight = weights[pl.ds(first * input_count, depth), first * columns:(first + group) * columns]
        for side in range(n_sketch):
            def body(at, total):
                start = pl.multiple_of(at * tile, tile)
                block = window[side, pl.ds(first, lag_total + group - 1), :, pl.ds(start, tile)]
                product = lax.dot_general(
                    block.reshape(depth, tile), weight, (((0,), (0,)), ((), ())),
                    preferred_element_type=jnp.float32,
                )
                for row in range(group):
                    part = product[:, row * columns:(row + 1) * columns]
                    raw[first + row, pl.ds(side * half + start, tile), :] = part
                    total = total + jnp.sum((part * part).reshape(tile // 8, 8, columns), axis=0)
                return total
            total = lax.fori_loop(0, half // tile, body, total, unroll=depth <= 512)
        return total

    own.wait()
    total = jnp.zeros((8, columns), jnp.float32)
    done = 0
    paired = False
    for first in range(0, step_count, group):
        need = first + group - 1 + lag_total
        ready = done
        while ready < len(pieces) and pieces[ready][0] * step_count + pieces[ready][1] < need:
            forward(ready)
            ready += 1
        if not paired:
            for index in range(n_sketch - 1):
                pair_copy(index).wait()
            paired = True
        for number in range(done, ready):
            landed(number)
        done = ready
        total = compute(first, total)

    sums[pl.ds(flat, 1), :] = jnp.sum(total, axis=0, keepdims=True)

    def sum_copy(index):
        place = sums.at[pl.ds(flat, 1)]
        return pltpu.make_async_remote_copy(
            src_ref=place,
            dst_ref=place,
            send_sem=sum_send,
            recv_sem=sum_recv,
            device_id=peer(index),
            device_id_type=MESH,
        )

    loop(peers, lambda index: sum_copy(index).start())
    for number in range(len(pieces)):
        @pl.when(lag >= pieces[number][0])
        def _():
            lag_copy(number).wait_send()
    if peers:
        arrived = sums.at[pl.ds(0, peers)]
        pltpu.make_async_copy(arrived, arrived, sum_recv).wait()
        pltpu.make_async_copy(arrived, arrived, sum_send).wait()
    cells = step_count * n_lag * half * n_sketch * n_probe
    mean = jnp.sum(sums[...], axis=0, keepdims=True) / cells
    factor[...] = jnp.broadcast_to(lax.rsqrt(mean + 1e-06), factor.shape)


def scale_kernel(raw, factor, out, held, sem):
    step_count, probes, columns = raw.shape
    pieces = 2
    part = probes // pieces
    copies = []
    gain = factor[0:1, :]
    for row in range(step_count):
        for piece in range(pieces):
            place = pl.ds(piece * part, part)
            held[row, place] = (raw[row, place] * gain).astype(held.dtype)
            copy = pltpu.make_async_copy(
                held.at[row, place], out.at[row, place], sem.at[row * pieces + piece]
            )
            copy.start()
            copies.append(copy)
    for copy in copies:
        copy.wait()


def scale(raw, factor):
    step_count, probes, columns = raw.shape
    return pl.pallas_call(
        scale_kernel,
        out_shape=jax.ShapeDtypeStruct(raw.shape, jnp.bfloat16),
        in_specs=[pl.BlockSpec(memory_space=pltpu.VMEM)] * 2,
        out_specs=pl.BlockSpec(memory_space=pltpu.HBM),
        scratch_shapes=[
            pltpu.VMEM(raw.shape, jnp.bfloat16),
            pltpu.SemaphoreType.DMA((step_count * 2,)),
        ],
        compiler_params=pltpu.CompilerParams(vmem_limit_bytes=16 * 1024 * 1024),
    )(raw, factor)


def local(sizes, markov, test_matrix):
    n_lag, n_probe, n_sketch = sizes
    step_count, input_count, half = markov.shape
    matrix_rows, _, columns = test_matrix.shape
    lag_total = matrix_rows * n_lag
    steps, pieces = plan(step_count, lag_total)
    count = max(len(pieces), 1)
    pairs = max(n_sketch - 1, 1)
    probes = half * n_sketch
    dma = pltpu.SemaphoreType.DMA
    raw, factor = pl.pallas_call(
        functools.partial(gather_kernel, sizes),
        out_shape=[
            pltpu.VMEM((step_count, probes, columns), jnp.float32),
            pltpu.VMEM((8, columns), jnp.float32),
        ],
        in_specs=[pl.BlockSpec(memory_space=pltpu.HBM)] * 2,
        out_specs=[pl.BlockSpec(memory_space=pltpu.VMEM)] * 2,
        scratch_shapes=[
            pltpu.VMEM((n_sketch, steps, input_count, half), jnp.bfloat16),
            pltpu.VMEM((lag_total, input_count, columns), jnp.bfloat16),
            pltpu.VMEM((steps * input_count, step_count * columns), jnp.bfloat16),
            pltpu.VMEM((n_lag * n_probe, columns), jnp.float32),
            dma, dma, dma, dma,
            dma((pairs,)), dma((pairs,)),
            dma((count,)), dma((count,)),
            dma((count, pairs)), dma((count, pairs)),
            dma, dma,
        ],
        compiler_params=pltpu.CompilerParams(
            collective_id=0, has_side_effects=True, vmem_limit_bytes=59 * 1024 * 1024
        ),
    )(markov, test_matrix)
    return scale(raw, factor)


def solution(mesh):
    sizes = tuple(mesh.shape[name] for name in ("lag", "probe", "sketch"))
    return jax.shard_map(
        functools.partial(local, sizes),
        mesh=mesh,
        in_specs=(P("lag", None, ("probe", "sketch")), P("lag", None, "sketch")),
        out_specs=P("lag", "probe", "sketch"),
        check_vma=False,
    )
```

```python
import functools

import jax
import jax.numpy as jnp
from jax import lax
from jax.experimental import pallas as pl
from jax.experimental.pallas import tpu as pltpu
from jax.sharding import PartitionSpec as P

MESH = pl.DeviceIdType.MESH
UNROLL = 32
TILES = 4


def loop(count, body):
    if count <= UNROLL:
        for index in range(count):
            body(index)
    else:
        def step(index, carry):
            body(index)
            return carry
        lax.fori_loop(0, count, step, 0)


def plan(step_count, lag_total):
    steps = step_count + lag_total - 1
    blocks = (steps - 1) // step_count
    pieces = []
    for ahead in range(1, blocks + 1):
        used = min(step_count, steps - ahead * step_count)
        if blocks == 1:
            pieces += [(ahead, at, 1) for at in range(used)]
        else:
            pieces.append((ahead, 0, used))
    return steps, pieces


def gather_kernel(
    sizes, markov, matrix, raw, factor,
    window, held, weights, sums,
    own_sem, matrix_own_sem, matrix_send, matrix_recv,
    pair_send, pair_recv, lag_send, lag_recv, next_send, next_recv, sum_send, sum_recv,
):
    n_lag, n_probe, n_sketch = sizes
    step_count, input_count, half = markov.shape
    matrix_rows = matrix.shape[0]
    columns = matrix.shape[2]
    lag_total = matrix_rows * n_lag
    steps, pieces = plan(step_count, lag_total)
    lag = lax.axis_index("lag")
    probe = lax.axis_index("probe")
    sketch = lax.axis_index("sketch")
    flat = lag * n_probe + probe
    peers = n_lag * n_probe - 1

    def peer(index):
        other = lax.rem(flat + 1 + index, peers + 1)
        return {
            "lag": lax.div(other, n_probe),
            "probe": lax.rem(other, n_probe),
            "sketch": sketch,
        }

    def partner(index):
        return {"lag": lag, "probe": probe, "sketch": lax.rem(sketch + 1 + index, n_sketch)}

    def lag_peer(index):
        return {"lag": lax.rem(lag + 1 + index, n_lag), "probe": probe, "sketch": sketch}

    barrier = pltpu.get_barrier_semaphore()

    def greet(index):
        pl.semaphore_signal(barrier, inc=1, device_id=peer(index), device_id_type=MESH)

    for index in range(n_sketch - 1):
        pl.semaphore_signal(barrier, inc=1, device_id=partner(index), device_id_type=MESH)
    loop(peers, greet)

    own = pltpu.make_async_copy(markov, window.at[sketch, pl.ds(0, step_count)], own_sem)
    own.start()
    matrix_own = pltpu.make_async_copy(
        matrix, held.at[pl.ds(lag * matrix_rows, matrix_rows)], matrix_own_sem
    )
    matrix_own.start()
    weights[...] = jnp.zeros_like(weights)
    for ahead, at, count in pieces:
        @pl.when(lag + ahead >= n_lag)
        def _():
            place = pl.ds(ahead * step_count + at, count)
            window[:, place] = jnp.zeros((n_sketch, count, input_count, half), window.dtype)

    pl.semaphore_wait(barrier, peers + n_sketch - 1)

    def lag_copy(number):
        ahead, at, count = pieces[number]
        return pltpu.make_async_remote_copy(
            src_ref=markov.at[pl.ds(at, count)],
            dst_ref=window.at[sketch, pl.ds(ahead * step_count + at, count)],
            send_sem=lag_send.at[number],
            recv_sem=lag_recv.at[number],
            device_id={"lag": lax.max(lag - ahead, 0), "probe": probe, "sketch": sketch},
            device_id_type=MESH,
        )

    def pair_copy(index):
        return pltpu.make_async_remote_copy(
            src_ref=markov,
            dst_ref=window.at[sketch, pl.ds(0, step_count)],
            send_sem=pair_send.at[index],
            recv_sem=pair_recv.at[index],
            device_id=partner(index),
            device_id_type=MESH,
        )

    def next_copy(number, index):
        ahead, at, count = pieces[number]
        place = window.at[sketch, pl.ds(ahead * step_count + at, count)]
        return pltpu.make_async_remote_copy(
            src_ref=place,
            dst_ref=place,
            send_sem=next_send.at[number, index],
            recv_sem=next_recv.at[number, index],
            device_id=partner(index),
            device_id_type=MESH,
        )

    def matrix_copy(index):
        return pltpu.make_async_remote_copy(
            src_ref=matrix,
            dst_ref=held.at[pl.ds(lag * matrix_rows, matrix_rows)],
            send_sem=matrix_send,
            recv_sem=matrix_recv,
            device_id=lag_peer(index),
            device_id_type=MESH,
        )

    loop(n_lag - 1, lambda index: matrix_copy(index).start())
    for number in range(0, 1):
        @pl.when(lag >= pieces[number][0])
        def _():
            lag_copy(number).start()
    for index in range(n_sketch - 1):
        pair_copy(index).start()
    for number in range(1, len(pieces)):
        @pl.when(lag >= pieces[number][0])
        def _():
            lag_copy(number).start()

    matrix_own.wait()
    if n_lag > 1:
        arrived = held.at[pl.ds(0, (n_lag - 1) * matrix_rows)]
        pltpu.make_async_copy(arrived, arrived, matrix_recv).wait()
        pltpu.make_async_copy(arrived, arrived, matrix_send).wait()
    for row in range(step_count):
        weights[pl.ds(row * input_count, lag_total * input_count), row * columns:(row + 1) * columns] = (
            held[...].reshape(lag_total * input_count, columns)
        )

    def forward(number):
        @pl.when(lag + pieces[number][0] < n_lag)
        def _():
            lag_copy(number).wait_recv()
            for index in range(n_sketch - 1):
                next_copy(number, index).start()

    def landed(number):
        @pl.when(lag + pieces[number][0] < n_lag)
        def _():
            for index in range(n_sketch - 1):
                next_copy(number, index).wait()

    tile = min(256, half)
    group = 2 if step_count % 2 == 0 else 1

    def compute(first, total):
        depth = (lag_total + group - 1) * input_count
        weight = weights[pl.ds(first * input_count, depth), first * columns:(first + group) * columns]
        for side in range(n_sketch):
            def body(at, total):
                start = pl.multiple_of(at * tile, tile)
                block = window[side, pl.ds(first, lag_total + group - 1), :, pl.ds(start, tile)]
                product = lax.dot_general(
                    block.reshape(depth, tile), weight, (((0,), (0,)), ((), ())),
                    preferred_element_type=jnp.float32,
                )
                for row in range(group):
                    part = product[:, row * columns:(row + 1) * columns]
                    raw[first + row, pl.ds(side * half + start, tile), :] = part
                    total = total + jnp.sum((part * part).reshape(tile // 8, 8, columns), axis=0)
                return total
            total = lax.fori_loop(0, half // tile, body, total, unroll=depth <= 512)
        return total

    own.wait()
    total = jnp.zeros((8, columns), jnp.float32)
    done = 0
    paired = False
    for first in range(0, step_count, group):
        need = first + group - 1 + lag_total
        ready = done
        while ready < len(pieces) and pieces[ready][0] * step_count + pieces[ready][1] < need:
            forward(ready)
            ready += 1
        if not paired:
            for index in range(n_sketch - 1):
                pair_copy(index).wait()
            paired = True
        for number in range(done, ready):
            landed(number)
        done = ready
        total = compute(first, total)

    sums[pl.ds(flat, 1), :] = jnp.sum(total, axis=0, keepdims=True)

    def sum_copy(index):
        place = sums.at[pl.ds(flat, 1)]
        return pltpu.make_async_remote_copy(
            src_ref=place,
            dst_ref=place,
            send_sem=sum_send,
            recv_sem=sum_recv,
            device_id=peer(index),
            device_id_type=MESH,
        )

    loop(peers, lambda index: sum_copy(index).start())
    for number in range(len(pieces)):
        @pl.when(lag >= pieces[number][0])
        def _():
            lag_copy(number).wait_send()
    if peers:
        arrived = sums.at[pl.ds(0, peers)]
        pltpu.make_async_copy(arrived, arrived, sum_recv).wait()
        pltpu.make_async_copy(arrived, arrived, sum_send).wait()
    cells = step_count * n_lag * half * n_sketch * n_probe
    mean = jnp.sum(sums[...], axis=0, keepdims=True) / cells
    factor[...] = jnp.broadcast_to(lax.rsqrt(mean + 1e-06), factor.shape)


def scale_kernel(raw, factor, out, held, sem):
    step_count, probes, columns = raw.shape
    pieces = 2
    part = probes // pieces
    copies = []
    gain = factor[0:1, :]
    for row in range(step_count):
        for piece in range(pieces):
            place = pl.ds(piece * part, part)
            held[row, place] = (raw[row, place] * gain).astype(held.dtype)
            copy = pltpu.make_async_copy(
                held.at[row, place], out.at[row, place], sem.at[row * pieces + piece]
            )
            copy.start()
            copies.append(copy)
    for copy in copies:
        copy.wait()


def scale(raw, factor):
    step_count, probes, columns = raw.shape
    return pl.pallas_call(
        scale_kernel,
        out_shape=jax.ShapeDtypeStruct(raw.shape, jnp.bfloat16),
        in_specs=[pl.BlockSpec(memory_space=pltpu.VMEM)] * 2,
        out_specs=pl.BlockSpec(memory_space=pltpu.HBM),
        scratch_shapes=[
            pltpu.VMEM(raw.shape, jnp.bfloat16),
            pltpu.SemaphoreType.DMA((step_count * 2,)),
        ],
        compiler_params=pltpu.CompilerParams(vmem_limit_bytes=16 * 1024 * 1024),
    )(raw, factor)


def mirror_kernel(
    sizes, markov, matrix, raw, factor,
    window, held, weights, acc, sums,
    own_sem, matrix_own_sem, matrix_send, matrix_recv,
    pair_send, pair_recv, down_send, down_recv, up_send, up_recv,
    down_pair_send, down_pair_recv, up_pair_send, up_pair_recv,
    sum_send, sum_recv, known,
):
    n_lag, n_probe, n_sketch = sizes
    step_count, input_count, half = markov.shape
    matrix_rows = matrix.shape[0]
    columns = matrix.shape[2]
    lag_total = matrix_rows * n_lag
    tail = lag_total - 1
    alone = step_count - tail
    tile = half // TILES
    early = TILES // 2
    lag = lax.axis_index("lag")
    probe = lax.axis_index("probe")
    sketch = lax.axis_index("sketch")
    flat = lag * n_probe + probe
    peers = n_lag * n_probe - 1
    has_next = lag < n_lag - 1
    has_back = lag > 0

    def peer(index):
        other = lax.rem(flat + 1 + index, peers + 1)
        return {
            "lag": lax.div(other, n_probe),
            "probe": lax.rem(other, n_probe),
            "sketch": sketch,
        }

    def partner(index):
        return {"lag": lag, "probe": probe, "sketch": lax.rem(sketch + 1 + index, n_sketch)}

    def lag_peer(index):
        return {"lag": lax.rem(lag + 1 + index, n_lag), "probe": probe, "sketch": sketch}

    def probe_peer(index):
        return {"lag": lag, "probe": lax.rem(probe + 1 + index, n_probe), "sketch": sketch}

    barrier = pltpu.get_barrier_semaphore()
    near = (
        [partner(index) for index in range(n_sketch - 1)]
        + [lag_peer(index) for index in range(n_lag - 1)]
        + [probe_peer(index) for index in range(n_probe - 1)]
    )
    for device in near:
        pl.semaphore_signal(barrier, inc=1, device_id=device, device_id_type=MESH)

    own = pltpu.make_async_copy(markov, window.at[sketch, pl.ds(tail, step_count)], own_sem)
    own.start()
    matrix_own = pltpu.make_async_copy(
        matrix, held.at[pl.ds(lag * matrix_rows, matrix_rows)], matrix_own_sem
    )
    matrix_own.start()
    weights[...] = jnp.zeros_like(weights)
    acc[...] = jnp.zeros_like(acc)

    @pl.when(lag == n_lag - 1)
    def _():
        window[:, pl.ds(tail + step_count, tail)] = jnp.zeros(
            (n_sketch, tail, input_count, half), window.dtype
        )

    pl.semaphore_wait(barrier, len(near))
    for index in range(n_lag - 1):
        pl.semaphore_signal(known, inc=1, device_id=lag_peer(index), device_id_type=MESH)

    def spot(first, count, number):
        return window.at[sketch, pl.ds(first, count), :, pl.ds(number * tile, tile)]

    def remote(source, target, send, recv, device):
        return pltpu.make_async_remote_copy(
            src_ref=source, dst_ref=target, send_sem=send, recv_sem=recv,
            device_id=device, device_id_type=MESH,
        )

    def down(number):
        return remote(
            markov.at[pl.ds(0, tail), :, pl.ds(number * tile, tile)],
            spot(tail + step_count, tail, number),
            down_send.at[number], down_recv.at[number],
            {"lag": lax.max(lag - 1, 0), "probe": probe, "sketch": sketch},
        )

    def up(number):
        return remote(
            markov.at[pl.ds(alone, tail), :, pl.ds(number * tile, tile)],
            spot(0, tail, number),
            up_send.at[number], up_recv.at[number],
            {"lag": lax.min(lag + 1, n_lag - 1), "probe": probe, "sketch": sketch},
        )

    def pair(index):
        return remote(
            markov, window.at[sketch, pl.ds(tail, step_count)],
            pair_send.at[index], pair_recv.at[index], partner(index),
        )

    def down_pair(number, index):
        place = spot(tail + step_count, tail, number)
        return remote(
            place, place, down_pair_send.at[number, index], down_pair_recv.at[number, index],
            partner(index),
        )

    def up_pair(number, index):
        place = spot(0, tail, number)
        return remote(
            place, place, up_pair_send.at[number, index], up_pair_recv.at[number, index],
            partner(index),
        )

    def matrix_copy(index):
        return remote(
            matrix, held.at[pl.ds(lag * matrix_rows, matrix_rows)],
            matrix_send, matrix_recv, lag_peer(index),
        )

    for index in range(n_lag - 1):
        matrix_copy(index).start()

    @pl.when(has_back)
    def _():
        for number in range(early):
            down(number).start()

    @pl.when(has_next)
    def _():
        for number in range(early, TILES):
            up(number).start()

    for index in range(n_sketch - 1):
        pair(index).start()

    @pl.when(has_back)
    def _():
        for number in range(early, TILES):
            down(number).start()

    matrix_own.wait()
    arrived = held.at[pl.ds(0, (n_lag - 1) * matrix_rows)]
    pltpu.make_async_copy(arrived, arrived, matrix_recv).wait()
    pltpu.make_async_copy(arrived, arrived, matrix_send).wait()
    for row in range(step_count):
        weights[pl.ds(row * input_count, lag_total * input_count), row * columns:(row + 1) * columns] = (
            held[...].reshape(lag_total * input_count, columns)
        )

    def compute(place, first, rows, side, start, width, stored, summed):
        depth = (lag_total + rows - 1) * input_count
        block = window[side, pl.ds(place, lag_total + rows - 1), :, pl.ds(start, width)]
        product = lax.dot_general(
            block.reshape(depth, width), weights[pl.ds(0, depth), 0:rows * columns],
            (((0,), (0,)), ((), ())), preferred_element_type=jnp.float32,
        )
        total = jnp.zeros((8, columns), jnp.float32)
        for row in range(rows):
            part = product[:, row * columns:(row + 1) * columns]
            if stored:
                raw[first + row, pl.ds(side * half + start, width), :] = part
            if summed:
                total = total + jnp.sum((part * part).reshape(width // 8, 8, columns), axis=0)
        if summed:
            acc[...] += total

    def forward_down(number):
        @pl.when(has_next)
        def _():
            down(number).wait_recv()
            for index in range(n_sketch - 1):
                down_pair(number, index).start()

    def forward_up(number):
        @pl.when(has_back)
        def _():
            up(number).wait_recv()
            for index in range(n_sketch - 1):
                up_pair(number, index).start()

    def own_rows(side, number, summed):
        compute(tail + alone, alone, tail, side, number * tile, tile, True, summed)

    own.wait()
    for number in range(early):
        forward_down(number)
        forward_up(early + number)
    for index in range(n_sketch - 1):
        pair(index).wait()
    for side in range(n_sketch):
        for number in range(TILES):
            compute(tail, 0, alone, side, number * tile, tile, True, True)
    for number in range(early):
        @pl.when(has_next)
        def _():
            for index in range(n_sketch - 1):
                down_pair(number, index).wait()
        for side in range(n_sketch):
            own_rows(side, number, True)

        @pl.when(has_back)
        def _():
            for index in range(n_sketch - 1):
                up_pair(early + number, index).wait()
            for side in range(n_sketch):
                compute(0, alone, tail, side, (early + number) * tile, tile, False, True)

    @pl.when(lag == n_lag - 1)
    def _():
        for side in range(n_sketch):
            for number in range(early, TILES):
                own_rows(side, number, True)

    sums[pl.ds(flat, 1), :] = jnp.sum(acc[...], axis=0, keepdims=True)

    def sum_copy(index):
        place = sums.at[pl.ds(flat, 1)]
        return remote(place, place, sum_send, sum_recv, peer(index))

    pl.semaphore_wait(known, n_lag - 1)
    for index in range(peers):
        sum_copy(index).start()

    for number in range(early, TILES):
        forward_down(number)

    @pl.when(has_next)
    def _():
        for number in range(early, TILES):
            for index in range(n_sketch - 1):
                down_pair(number, index).wait()
            for side in range(n_sketch):
                own_rows(side, number, False)
        for number in range(early, TILES):
            up(number).wait_send()

    @pl.when(has_back)
    def _():
        for number in range(TILES):
            down(number).wait_send()

    arrived = sums.at[pl.ds(0, peers)]
    pltpu.make_async_copy(arrived, arrived, sum_recv).wait()
    pltpu.make_async_copy(arrived, arrived, sum_send).wait()
    cells = step_count * n_lag * half * n_sketch * n_probe
    mean = jnp.sum(sums[...], axis=0, keepdims=True) / cells
    factor[...] = jnp.broadcast_to(lax.rsqrt(mean + 1e-06), factor.shape)


def mirrored(sizes, markov, test_matrix):
    n_lag, n_probe, n_sketch = sizes
    step_count, input_count, half = markov.shape
    matrix_rows, _, columns = test_matrix.shape
    lag_total = matrix_rows * n_lag
    tail = lag_total - 1
    pairs = max(n_sketch - 1, 1)
    dma = pltpu.SemaphoreType.DMA
    return pl.pallas_call(
        functools.partial(mirror_kernel, sizes),
        out_shape=[
            pltpu.VMEM((step_count, half * n_sketch, columns), jnp.float32),
            pltpu.VMEM((8, columns), jnp.float32),
        ],
        in_specs=[pl.BlockSpec(memory_space=pltpu.HBM)] * 2,
        out_specs=[pl.BlockSpec(memory_space=pltpu.VMEM)] * 2,
        scratch_shapes=[
            pltpu.VMEM((n_sketch, step_count + 2 * tail, input_count, half), jnp.bfloat16),
            pltpu.VMEM((lag_total, input_count, columns), jnp.bfloat16),
            pltpu.VMEM(((step_count + tail) * input_count, step_count * columns), jnp.bfloat16),
            pltpu.VMEM((8, columns), jnp.float32),
            pltpu.VMEM((n_lag * n_probe, columns), jnp.float32),
            dma, dma, dma, dma,
            dma((pairs,)), dma((pairs,)),
            dma((TILES,)), dma((TILES,)), dma((TILES,)), dma((TILES,)),
            dma((TILES, pairs)), dma((TILES, pairs)), dma((TILES, pairs)), dma((TILES, pairs)),
            dma, dma, pltpu.SemaphoreType.REGULAR,
        ],
        compiler_params=pltpu.CompilerParams(
            collective_id=1, has_side_effects=True, vmem_limit_bytes=59 * 1024 * 1024
        ),
    )(markov, test_matrix)


def local(sizes, markov, test_matrix):
    n_lag, n_probe, n_sketch = sizes
    step_count, input_count, half = markov.shape
    matrix_rows, _, columns = test_matrix.shape
    lag_total = matrix_rows * n_lag
    if 1 < lag_total <= step_count and n_lag > 1 and half % (128 * TILES) == 0:
        return scale(*mirrored(sizes, markov, test_matrix))
    steps, pieces = plan(step_count, lag_total)
    count = max(len(pieces), 1)
    pairs = max(n_sketch - 1, 1)
    probes = half * n_sketch
    dma = pltpu.SemaphoreType.DMA
    raw, factor = pl.pallas_call(
        functools.partial(gather_kernel, sizes),
        out_shape=[
            pltpu.VMEM((step_count, probes, columns), jnp.float32),
            pltpu.VMEM((8, columns), jnp.float32),
        ],
        in_specs=[pl.BlockSpec(memory_space=pltpu.HBM)] * 2,
        out_specs=[pl.BlockSpec(memory_space=pltpu.VMEM)] * 2,
        scratch_shapes=[
            pltpu.VMEM((n_sketch, steps, input_count, half), jnp.bfloat16),
            pltpu.VMEM((lag_total, input_count, columns), jnp.bfloat16),
            pltpu.VMEM((steps * input_count, step_count * columns), jnp.bfloat16),
            pltpu.VMEM((n_lag * n_probe, columns), jnp.float32),
            dma, dma, dma, dma,
            dma((pairs,)), dma((pairs,)),
            dma((count,)), dma((count,)),
            dma((count, pairs)), dma((count, pairs)),
            dma, dma,
        ],
        compiler_params=pltpu.CompilerParams(
            collective_id=0, has_side_effects=True, vmem_limit_bytes=59 * 1024 * 1024
        ),
    )(markov, test_matrix)
    return scale(raw, factor)


def solution(mesh):
    sizes = tuple(mesh.shape[name] for name in ("lag", "probe", "sketch"))
    return jax.shard_map(
        functools.partial(local, sizes),
        mesh=mesh,
        in_specs=(P("lag", None, ("probe", "sketch")), P("lag", None, "sketch")),
        out_specs=P("lag", "probe", "sketch"),
        check_vma=False,
    )
```
